256 devices in a mesh: pool: 32 (over y_lo, z, core), tensor: 8 (over x, y_hi).
Axes of the slice: x: 4, y: 4 (y_hi: 2, y_lo: 2; y = y_hi * 2 + y_lo), z: 8, core: 2. Of those that a mesh axis runs over, the one named last changes fastest.
Arguments:
- saved_rows: bfloat16 [65536, 5120], P('pool', 'tensor'), may hold values from -800 to 800
- norm_gain: bfloat16 [5120], replicated, may hold values from 0.099609375 to 1.8984375
- w_key: bfloat16 [5120, 3072], P('pool', 'tensor'), may hold values from -0.078125 to 0.078125
- w_value: bfloat16 [5120, 3072], P('pool', 'tensor'), may hold values from -0.078125 to 0.078125
- req_blocks: int32 [16], replicated, may hold values from 1 to 14, 208 in all
- req_tail: int32 [16], replicated, may hold values from 1 to 128
- group_request: int32 [32], replicated, may hold values from 0 to 31, each once
- owner_table: int32 [16, 14], replicated, may hold values from 0 to 31, as said below
- new_hidden: bfloat16 [128, 2, 5120], P('pool', None, 'tensor'), may hold values from -800 to 800
- queries: bfloat16 [128, 2, 3072], P('pool', None, 'tensor'), may hold values from -200 to 200
- cache_key: bfloat16 [128, 1024, 3072], P('pool', None, 'tensor'), may hold values from -5 to 5
- cache_value: bfloat16 [128, 1024, 3072], P('pool', None, 'tensor'), may hold values from -4 to 4
- cache_len: int32 [128], P('pool'), may hold values from 2 to 1022, as said below
Outputs:
- restored_key: bfloat16 [57344, 3072], P('pool', 'tensor')
- restored_value: bfloat16 [57344, 3072], P('pool', 'tensor')
- decode_out: bfloat16 [128, 2, 3072], P('pool', None, 'tensor')
- new_key: bfloat16 [128, 2, 3072], P('pool', None, 'tensor')
- new_value: bfloat16 [128, 2, 3072], P('pool', None, 'tensor')
The draws below stay inside these ranges and needn't reach their ends.
Inputs may be any that keep to these rules, and one draw needn't show every extreme that they name: `req_blocks`: they sum to 208; the largest is exactly 14. Each number once; group g restores request group_request[g] when it is below 16, else none. Block i of request r (i < req_blocks[r]) is kept by pool index owner_table[r, i] in its slot r; the numbers of one row differ; entries at i >= req_blocks[r] are unused. `cache_len`: some request has exactly 1022.
All inputs are finite; a program needn't handle non-finite values.
Results may differ from the reference program's by a relative error of at most 0.0056.
Values may be sent and summed in bfloat16 or wider, within the bound.
No kernel may reach another device: no remote copies, remote signals or barrier semaphores. Data moves between devices by JAX's collectives and lax.ppermute only.
A program may use at most 128 MiB of HBM per device.

```python
import math
import jax
import jax.numpy as jnp
import numpy as np
from jax import lax

D = 5120
HEAD_DIM = 128
HEADS = 24
REQS = 16
BLOCK = 128
BLOCKS = 208
GBLK = 14
STEPS = 2
CTX = 1024
RES = 128
N_POOL = 32


def scaled_field(key, count, features):
    noise_key, row_key, column_key = jax.random.split(key, 3)
    field = jnp.clip(jax.random.normal(noise_key, (count, features), jnp.float32), -4.0, 4.0)
    row_scale = 10.0 ** jax.random.uniform(row_key, (count, 1), jnp.float32)
    column_rise = jnp.arange(features, dtype=jnp.float32)[None, :] / features * 0.5
    column_scale = 10.0 ** (column_rise + 0.5 * jax.random.uniform(column_key, (1, features), jnp.float32))
    return row_scale * column_scale * field


def shared_keys(key):
    return jnp.clip(jax.random.normal(key, (RES, CTX, HEADS * HEAD_DIM), jnp.float32), -4.0, 4.0)


def draw_saved_rows(key, part):
    key = jax.random.fold_in(key, 11)
    return scaled_field(key, N_POOL * REQS * BLOCK, D).astype(jnp.bfloat16)


def draw_new_hidden(key, part):
    key = jax.random.fold_in(key, 12)
    field = scaled_field(key, RES * STEPS, D)
    return field.reshape(RES, STEPS, D).astype(jnp.bfloat16)


def draw_cache_key(key, part):
    cached = shared_keys(key)
    return cached.astype(jnp.bfloat16)


def draw_queries(key, part):
    key = jax.random.fold_in(key, 14)
    normal_key = jax.random.fold_in(key, 0)
    fresh = jnp.clip(jax.random.normal(normal_key, (RES, STEPS, HEADS * HEAD_DIM), jnp.float32), -4.0, 4.0)
    return fresh.astype(jnp.bfloat16)


def draw_cache_len(key, part):
    key = jax.random.fold_in(key, 15)
    level_key, offset_key, pick_key = jax.random.split(key, 3)
    top_level = CTX.bit_length() - 1
    levels = jax.random.randint(level_key, (RES,), 1, top_level + 1)
    span = jnp.left_shift(jnp.ones((RES,), jnp.int32), levels)
    offsets = jax.random.randint(offset_key, (RES,), 0, 1 << 20)
    counts = 2 + offsets % (span - 1)
    counts = jnp.minimum(counts, CTX - STEPS)
    pick = jax.random.randint(pick_key, (), 0, RES)
    counts = counts.at[pick].set(CTX - STEPS)
    return counts.astype(jnp.int32)


def draw_owner_table(key, part):
    key = jax.random.fold_in(key, 16)
    row_keys = jax.random.split(key, REQS)

    def one_row(row_key):
        return jax.random.permutation(row_key, N_POOL)
    orders = jax.vmap(one_row)(row_keys)
    return orders[:, :GBLK].astype(jnp.int32)


def plant(result, rng, low, largest):
    extent = result.shape
    spot = [jax.random.randint(jax.random.fold_in(rng, axis), (), 0, extent[axis]) for axis in range(len(extent))]
    result = result.at[tuple(spot)].set(low)
    longest = extent.index(max(extent))
    spot[longest] = (spot[longest] + 1) % extent[longest]
    return result.at[tuple(spot)].set(largest)


def level_of(own_key, extent, pieces, smallest, largest):
    level, own = 1.0, jax.random.fold_in(own_key, 6)
    for dim, blocks in pieces:
        steps = jnp.exp(jax.random.uniform(jax.random.fold_in(own, dim), (blocks,), jnp.float32, smallest / len(pieces), largest / len(pieces)))
        level = level * jnp.repeat(steps, extent[dim] // blocks).reshape([-1 if axis == dim else 1 for axis in range(len(extent))])
    return level


def split_up(number_of, total, most, lean):
    portions = [(1 << 20) // math.isqrt(standing ** lean) + 1 for standing in range(2, number_of + 1)]
    surplus, given = total - most - (number_of - 1), [1] * (number_of - 1)
    while surplus > 0:
        candidates = [i for i in range(number_of - 1) if given[i] < most]
        pool, budget = sum([portions[i] for i in candidates]), surplus
        for i in candidates:
            extra = min(most - given[i], max(1, budget * portions[i] // pool), surplus)
            given[i] = given[i] + extra
            surplus = surplus - extra
    return np.array([most] + given)


def uneven(rng, amount, total, reach, slope):
    if amount == 2:
        one = jax.random.randint(rng, (), max(1, total - reach), min(reach, total - 1) + 1)
        return jnp.stack([one, total - one])
    tallies = jnp.asarray(split_up(amount, total, reach, slope), jnp.int32)
    pairs = (amount - 1) // 2
    giver, receiver = tallies[1:1 + 2 * pairs:2], tallies[2:2 + 2 * pairs:2]
    margin = jnp.minimum(giver - 1, reach - receiver)
    moved = jax.random.randint(jax.random.fold_in(rng, 1), (pairs,), 0, 1 << 20) % (margin + 1)
    tallies = tallies.at[1:1 + 2 * pairs:2].set(giver - moved).at[2:2 + 2 * pairs:2].set(receiver + moved)
    return tallies[jax.random.permutation(jax.random.fold_in(rng, 2), amount)]


def normal_values(stream_key, shape, scale, bound, shards=(), held_as=jnp.bfloat16):
    values = scale * jax.random.normal(stream_key, shape, jnp.float32)
    if shards:
        values = values * level_of(stream_key, shape, shards, -0.22, 0.18)
    return jnp.clip(values, -bound, bound).astype(held_as)


def setup_inputs(seed: int = 0) -> dict:
    key_list = jax.random.split(jax.random.key(seed), 14)
    return {
        "saved_rows": draw_saved_rows(jax.random.fold_in(key_list[13], 71), 0),
        "norm_gain": jnp.clip(1.0 + 0.18 * jax.random.normal(key_list[1], (D,), jnp.float32), 0.099609375, 1.8984375).astype(jnp.bfloat16),
        "w_key": normal_values(key_list[2], (D, HEADS * HEAD_DIM), D ** -0.5, 0.078125, ((0, 32), (1, 8))),
        "w_value": normal_values(key_list[3], (D, HEADS * HEAD_DIM), D ** -0.5, 0.078125, ((0, 32), (1, 8))),
        "req_blocks": uneven(key_list[4], REQS, BLOCKS, GBLK, 2).astype(jnp.int32),
        "req_tail": plant(jax.random.randint(key_list[5], (REQS,), 1, BLOCK + 1), jax.random.fold_in(key_list[5], 1), 1, BLOCK).astype(jnp.int32),
        "group_request": jax.random.permutation(key_list[6], N_POOL).astype(jnp.int32),
        "owner_table": draw_owner_table(jax.random.fold_in(key_list[13], 71), 0),
        "new_hidden": draw_new_hidden(jax.random.fold_in(key_list[13], 71), 0),
        "queries": draw_queries(jax.random.fold_in(key_list[13], 71), 0),
        "cache_key": draw_cache_key(jax.random.fold_in(key_list[13], 71), 0),
        "cache_value": normal_values(key_list[11], (RES, CTX, HEADS * HEAD_DIM), 1.0, 4.0, ((0, 32), (2, 8))),
        "cache_len": draw_cache_len(jax.random.fold_in(key_list[13], 71), 0),
    }


epsilon = 1e-05

def rotate(values, positions):
    head_count = values.shape[-1] // HEAD_DIM
    half_dim = HEAD_DIM // 2
    shaped = values.reshape(values.shape[:-1] + (head_count, HEAD_DIM))
    frequency = 10000.0 ** (-2.0 * jnp.arange(half_dim, dtype=jnp.float32) / HEAD_DIM)
    angle_rows = positions.astype(jnp.float32)[..., None] * frequency
    cosine = jnp.cos(angle_rows)[..., None, :]
    sine_part = jnp.sin(angle_rows)[..., None, :]
    first_half = shaped[..., :half_dim]
    second = shaped[..., half_dim:]
    turned = jnp.concatenate([first_half * cosine - second * sine_part, second * cosine + first_half * sine_part], axis=-1)
    return turned.reshape(values.shape)

def project(source_rows, norm_gain, w_key, w_value):
    wide_rows = source_rows.astype(jnp.float32)
    inverse = lax.rsqrt(lax.optimization_barrier(jnp.sum(wide_rows * wide_rows, axis=-1)) / D + epsilon)
    scaled = (wide_rows * norm_gain.astype(jnp.float32)).astype(jnp.bfloat16)
    key_raw = jnp.dot(scaled, w_key, preferred_element_type=jnp.float32) * inverse[:, None]
    value_raw = jnp.dot(scaled, w_value, preferred_element_type=jnp.float32) * inverse[:, None]
    return (key_raw, value_raw)

def reference(saved_rows, norm_gain, w_key, w_value, req_blocks, req_tail, group_request, owner_table, new_hidden, queries, cache_key, cache_value, cache_len):

    def restore_one(request):
        owners = owner_table[request]
        row_base = (owners * REQS + request) * BLOCK
        row_index = (row_base[:, None] + jnp.arange(BLOCK, dtype=jnp.int32)[None, :]).reshape(-1).astype(jnp.int32)
        picked = jnp.take(saved_rows, row_index, axis=0)
        token_count = (req_blocks[request] - 1) * BLOCK + req_tail[request]
        position = jnp.arange(GBLK * BLOCK, dtype=jnp.int32)
        live_rows = position < token_count
        picked = jnp.where(live_rows[:, None], picked, jnp.zeros((), jnp.bfloat16))
        key_raw, value_raw = project(picked, norm_gain, w_key, w_value)
        return (rotate(key_raw, position).astype(jnp.bfloat16), value_raw.astype(jnp.bfloat16))
    key_rows, value_rows = lax.map(restore_one, jnp.arange(REQS, dtype=jnp.int32))
    present = group_request < REQS
    chosen = jnp.minimum(group_request, REQS - 1).astype(jnp.int32)
    restored_key = jnp.where(present[:, None, None], jnp.take(key_rows, chosen, axis=0), jnp.zeros((), jnp.bfloat16))
    restored_value = jnp.where(present[:, None, None], jnp.take(value_rows, chosen, axis=0), jnp.zeros((), jnp.bfloat16))
    restored_key = restored_key.reshape(N_POOL * GBLK * BLOCK, HEADS * HEAD_DIM).astype(jnp.bfloat16)
    restored_value = restored_value.reshape(N_POOL * GBLK * BLOCK, HEADS * HEAD_DIM).astype(jnp.bfloat16)

    def decode_one(packed):
        hidden_rows, query_rows, cached_key, cached_value, token_count = packed
        key_raw, value_raw = project(hidden_rows, norm_gain, w_key, w_value)
        positions = token_count + jnp.arange(STEPS, dtype=jnp.int32)
        fresh_key = rotate(key_raw, positions).astype(jnp.bfloat16)
        fresh_value = value_raw.astype(jnp.bfloat16)
        score_scale = HEAD_DIM ** (-0.5)
        query_heads = query_rows.astype(jnp.float32).reshape(STEPS, HEADS, HEAD_DIM)
        cached_heads = cached_key.astype(jnp.float32).reshape(CTX, HEADS, HEAD_DIM)
        cached_scores = jnp.einsum('shd,chd->shc', query_heads, cached_heads) * score_scale
        cached_scores = jnp.where(jnp.arange(CTX)[None, None, :] < token_count, cached_scores, -1e+30)
        fresh_heads = fresh_key.astype(jnp.float32).reshape(STEPS, HEADS, HEAD_DIM)
        fresh_scores = jnp.einsum('shd,thd->sht', query_heads, fresh_heads) * score_scale
        causal_mask = jnp.arange(STEPS)[None, :] <= jnp.arange(STEPS)[:, None]
        fresh_scores = jnp.where(causal_mask[:, None, :], fresh_scores, -1e+30)
        peak_score = jnp.maximum(lax.optimization_barrier(jnp.max(cached_scores, axis=-1)), lax.optimization_barrier(jnp.max(fresh_scores, axis=-1)))
        cached_terms = jnp.exp(cached_scores - peak_score[..., None])
        fresh_terms = jnp.exp(fresh_scores - peak_score[..., None])
        weight_sum = lax.optimization_barrier(jnp.sum(cached_terms, axis=-1)) + lax.optimization_barrier(jnp.sum(fresh_terms, axis=-1))
        cached_weights = (cached_terms / weight_sum[..., None]).astype(jnp.bfloat16)
        fresh_weights = (fresh_terms / weight_sum[..., None]).astype(jnp.bfloat16)
        cached_values = cached_value.astype(jnp.float32).reshape(CTX, HEADS, HEAD_DIM)
        fresh_values = fresh_value.astype(jnp.float32).reshape(STEPS, HEADS, HEAD_DIM)
        output = jnp.einsum('shc,chd->shd', cached_weights.astype(jnp.float32), cached_values)
        output = output + jnp.einsum('sht,thd->shd', fresh_weights.astype(jnp.float32), fresh_values)
        return (output.reshape(STEPS, HEADS * HEAD_DIM).astype(jnp.bfloat16), fresh_key, fresh_value)
    decode_out, new_key, new_value = lax.map(decode_one, (new_hidden, queries, cache_key, cache_value, cache_len))
    return (restored_key, restored_value, decode_out, new_key, new_value)
```

```python
import jax
import jax.numpy as jnp
from jax import lax
from jax.sharding import PartitionSpec as P

D = 5120
HEAD_DIM = 128
REQS = 16
BLOCK = 128
BLOCKS = 208
GBLK = 14
N_POOL = 32
N_TENSOR = 8
SHARE = BLOCK // N_POOL
ROWS = BLOCKS * SHARE
PART_A = 352


epsilon = 1e-05


def turn_table(positions):
    half_dim = HEAD_DIM // 2
    frequency = 10000.0 ** (-2.0 * jnp.arange(half_dim, dtype=jnp.float32) / HEAD_DIM)
    angle_rows = positions.astype(jnp.float32)[..., None] * frequency
    return jnp.cos(angle_rows), jnp.sin(angle_rows)


def rotate(values, positions):
    head_count = values.shape[-1] // HEAD_DIM
    half_dim = HEAD_DIM // 2
    cosine, sine_part = turn_table(positions)
    heads = []
    for head in range(head_count):
        first_half = values[..., head * HEAD_DIM : head * HEAD_DIM + half_dim]
        second = values[..., head * HEAD_DIM + half_dim : (head + 1) * HEAD_DIM]
        heads.append(first_half * cosine - second * sine_part)
        heads.append(second * cosine + first_half * sine_part)
    return jnp.concatenate(heads, axis=-1)


def attend(queries, cache_key, cache_value, fresh_key, fresh_value, cache_len):
    local_count, step_count, feature_count = queries.shape
    head_count = feature_count // HEAD_DIM
    context = cache_key.shape[1]
    score_scale = HEAD_DIM ** (-0.5)
    query_heads = queries.reshape(local_count, step_count, head_count, HEAD_DIM)
    cached_heads = cache_key.reshape(local_count, context, head_count, HEAD_DIM)
    cached_scores = (
        jnp.einsum("rshd,rchd->rshc", query_heads, cached_heads, preferred_element_type=jnp.float32)
        * score_scale
    )
    cached_scores = jnp.where(
        jnp.arange(context)[None, None, None, :] < cache_len[:, None, None, None],
        cached_scores,
        -1e30,
    )
    fresh_heads = fresh_key.reshape(local_count, step_count, head_count, HEAD_DIM)
    fresh_scores = (
        jnp.einsum("rshd,rthd->rsht", query_heads, fresh_heads, preferred_element_type=jnp.float32)
        * score_scale
    )
    causal_mask = jnp.arange(step_count)[None, :] <= jnp.arange(step_count)[:, None]
    fresh_scores = jnp.where(causal_mask[None, :, None, :], fresh_scores, -1e30)
    peak_score = jnp.maximum(jnp.max(cached_scores, axis=-1), jnp.max(fresh_scores, axis=-1))
    cached_terms = jnp.exp(cached_scores - peak_score[..., None])
    fresh_terms = jnp.exp(fresh_scores - peak_score[..., None])
    weight_sum = jnp.sum(cached_terms, axis=-1) + jnp.sum(fresh_terms, axis=-1)
    cached_weights = (cached_terms / weight_sum[..., None]).astype(jnp.bfloat16)
    fresh_weights = (fresh_terms / weight_sum[..., None]).astype(jnp.bfloat16)
    cached_values = cache_value.reshape(local_count, context, head_count, HEAD_DIM)
    fresh_values = fresh_value.reshape(local_count, step_count, head_count, HEAD_DIM)
    output = jnp.einsum(
        "rshc,rchd->rshd", cached_weights, cached_values, preferred_element_type=jnp.float32
    )
    output = output + jnp.einsum(
        "rsht,rthd->rshd", fresh_weights, fresh_values, preferred_element_type=jnp.float32
    )
    return output.reshape(local_count, step_count, feature_count).astype(jnp.bfloat16)


def pick_rows(index, table):
    chosen = (index[:, None] == jnp.arange(table.shape[0], dtype=jnp.int32)[None, :]).astype(jnp.bfloat16)
    return jnp.dot(chosen, table, preferred_element_type=jnp.float32).astype(jnp.bfloat16)


def along_x(values, step):
    pairs = [(s, ((s // 2 + step) % 4) * 2 + s % 2) for s in range(N_TENSOR)]
    return lax.ppermute(values, "tensor", pairs)


def across_y(values):
    return lax.ppermute(values, "tensor", [(s, s ^ 1) for s in range(N_TENSOR)])


def ring_x(values):
    half = values.shape[0] // 2
    before = along_x(values, 1)
    after = along_x(values, -1)
    far_first = along_x(before[:half], 1)
    far_second = along_x(after[half:], -1)
    return [values, before, after, jnp.concatenate([far_first, far_second], axis=0)]


def project(pieces, weights, gain_wide):
    slice_width = D // N_TENSOR
    total, squares = None, None
    for values, source in pieces:
        wide = values.astype(jnp.float32)
        gain = lax.dynamic_slice_in_dim(gain_wide, source * slice_width, slice_width)
        share = lax.dynamic_slice_in_dim(weights, source * slice_width, slice_width, axis=0)
        scaled = (wide * gain).astype(jnp.bfloat16)
        part = jnp.dot(scaled, share, preferred_element_type=jnp.float32)
        square = jnp.sum(wide * wide, axis=1)
        total = part if total is None else total + part
        squares = square if squares is None else squares + square
    return total, squares


def shards(
    saved_rows,
    norm_gain,
    w_key,
    w_value,
    req_blocks,
    req_tail,
    group_request,
    owner_table,
    new_hidden,
    queries,
    cache_key,
    cache_value,
    cache_len,
):
    slice_width = saved_rows.shape[1]
    head_width = w_key.shape[1]
    pool_index = lax.axis_index("pool")
    tensor_index = lax.axis_index("tensor")
    gain_wide = norm_gain.astype(jnp.float32)
    weights = lax.all_gather(jnp.concatenate([w_key, w_value], axis=1), "pool", axis=0, tiled=True)

    spread = saved_rows.reshape(REQS, N_POOL, SHARE, slice_width).transpose(1, 0, 2, 3)
    incoming = lax.all_to_all(
        spread.reshape(N_POOL, REQS * SHARE, slice_width), "pool", split_axis=0, concat_axis=0, tiled=True
    ).reshape(N_POOL * REQS * SHARE, slice_width)

    ends = jnp.cumsum(req_blocks)
    starts = ends - req_blocks
    rank = jnp.arange(ROWS, dtype=jnp.int32)
    block = rank // SHARE
    request = jnp.sum((block[:, None] >= ends[None, :]).astype(jnp.int32), axis=1)
    inner = block - starts[request]
    owner = owner_table[request, inner]
    position = inner * BLOCK + pool_index * SHARE + rank % SHARE
    live = position < (req_blocks[request] - 1) * BLOCK + req_tail[request]
    rows = pick_rows((owner * REQS + request) * SHARE + rank % SHARE, incoming)

    local_count, step_count = (new_hidden.shape[0], new_hidden.shape[1])
    tokens = local_count * step_count
    own = jnp.concatenate(
        [rows, new_hidden.reshape(tokens, slice_width), jnp.zeros((tokens, slice_width), jnp.bfloat16)], axis=0
    )
    x_index, y_index = tensor_index // 2, tensor_index % 2
    sources = [x_index, (x_index + 3) % 4, (x_index + 1) % 4, (x_index + 2) % 4]

    part_a, part_b = own[:PART_A], own[PART_A:]
    across_b = across_y(part_b)
    ring_a = ring_x(part_a)
    ring_b = ring_x(part_b)
    ring_c = ring_x(across_b)
    pieces_a, pieces_b = [], []
    for values, source in zip(ring_a, sources):
        pieces_a.append((values, source * 2 + y_index))
        pieces_a.append((across_y(values), source * 2 + 1 - y_index))
    for values, source in zip(ring_b, sources):
        pieces_b.append((values, source * 2 + y_index))
    for values, source in zip(ring_c, sources):
        pieces_b.append((values, source * 2 + 1 - y_index))
    sum_a, squares_a = project(pieces_a, weights, gain_wide)
    sum_b, squares_b = project(pieces_b, weights, gain_wide)
    both = jnp.concatenate([sum_a, sum_b], axis=0)
    inverse = lax.rsqrt(jnp.concatenate([squares_a, squares_b]) / D + epsilon)

    restored_inverse = jnp.where(live, inverse[:ROWS], 0.0)[:, None]
    restored = jnp.concatenate(
        [
            rotate(both[:ROWS, :head_width] * restored_inverse, position).astype(jnp.bfloat16),
            (both[:ROWS, head_width:] * restored_inverse).astype(jnp.bfloat16),
        ],
        axis=1,
    )
    present = group_request < REQS
    chosen = jnp.minimum(group_request, REQS - 1)
    slot_rows = GBLK * SHARE
    outgoing_index = starts[chosen][:, None] * SHARE + jnp.arange(slot_rows, dtype=jnp.int32)[None, :]
    filled = present[:, None] & (jnp.arange(slot_rows)[None, :] < req_blocks[chosen][:, None] * SHARE)
    outgoing = pick_rows(jnp.where(filled, outgoing_index, -1).reshape(-1), restored)
    arrived = lax.all_to_all(
        outgoing.reshape(N_POOL, slot_rows, 2 * head_width), "pool", split_axis=0, concat_axis=0, tiled=True
    )
    arrived = (
        arrived.reshape(N_POOL, GBLK, SHARE, 2 * head_width)
        .transpose(1, 0, 2, 3)
        .reshape(GBLK * BLOCK, 2 * head_width)
    )
    restored_key = arrived[:, :head_width]
    restored_value = arrived[:, head_width:]

    token_both = both[ROWS : ROWS + tokens] * inverse[ROWS : ROWS + tokens, None]
    token_both = token_both.reshape(local_count, step_count, 2 * head_width)
    positions = cache_len[:, None] + jnp.arange(step_count, dtype=jnp.int32)[None, :]
    new_key = rotate(token_both[..., :head_width], positions).astype(jnp.bfloat16)
    new_value = token_both[..., head_width:].astype(jnp.bfloat16)
    decode_out = attend(queries, cache_key, cache_value, new_key, new_value, cache_len)
    return (restored_key, restored_value, decode_out, new_key, new_value)


def solution(mesh):
    return jax.shard_map(
        shards,
        mesh=mesh,
        in_specs=(
            P("pool", "tensor"),
            P(),
            P("pool", "tensor"),
            P("pool", "tensor"),
            P(),
            P(),
            P(),
            P(),
            P("pool", None, "tensor"),
            P("pool", None, "tensor"),
            P("pool", None, "tensor"),
            P("pool", None, "tensor"),
            P("pool"),
        ),
        out_specs=(
            P("pool", "tensor"),
            P("pool", "tensor"),
            P("pool", None, "tensor"),
            P("pool", None, "tensor"),
            P("pool", None, "tensor"),
        ),
        check_vma=False,
    )
```

```python
import jax
import jax.numpy as jnp
from jax import lax
from jax.experimental import pallas as pl
from jax.experimental.pallas import tpu as pltpu
from jax.sharding import PartitionSpec as P

D = 5120
HEAD_DIM = 128
REQS = 16
BLOCK = 128
BLOCKS = 208
GBLK = 14
N_POOL = 32
N_TENSOR = 8
CHIPS = N_POOL // 2
UNIT = BLOCK // CHIPS
PAIRS = GBLK // 2
CHUNKS = ((0, 4), (4, 7))
PART_A = (160, 128)


epsilon = 1e-05


def rotate(values, cosine, sine_part):
    head_count = values.shape[-1] // HEAD_DIM
    heads = []
    for head in range(head_count):
        one = values[..., head * HEAD_DIM : (head + 1) * HEAD_DIM]
        heads.append(one * cosine + jnp.roll(one, HEAD_DIM // 2, axis=-1) * sine_part)
    return jnp.concatenate(heads, axis=-1)


def turn_table(positions):
    half_dim = HEAD_DIM // 2
    frequency = 10000.0 ** (-2.0 * jnp.arange(half_dim, dtype=jnp.float32) / HEAD_DIM)
    angle_rows = positions.astype(jnp.float32)[..., None] * frequency
    cosine, sine_part = jnp.cos(angle_rows), jnp.sin(angle_rows)
    return jnp.concatenate([cosine, cosine], axis=-1), jnp.concatenate([-sine_part, sine_part], axis=-1)


def finish_kernel(total_ref, inverse_ref, cosine_ref, sine_ref, out_ref):
    half = total_ref.shape[1] // 2
    inverse = inverse_ref[...]
    cosine, sine_part = cosine_ref[...], sine_ref[...]
    for low in range(0, half, HEAD_DIM):
        one = total_ref[:, low : low + HEAD_DIM] * inverse
        turned = one * cosine + pltpu.roll(one, HEAD_DIM // 2, 1) * sine_part
        out_ref[:, low : low + HEAD_DIM] = turned.astype(jnp.bfloat16)
    out_ref[:, half:] = (total_ref[:, half:] * inverse).astype(jnp.bfloat16)


def finish(total, inverse, cosine, sine_part):
    rows, columns = total.shape
    return pl.pallas_call(
        finish_kernel,
        out_shape=jax.ShapeDtypeStruct((rows, columns), jnp.bfloat16),
        compiler_params=pltpu.CompilerParams(vmem_limit_bytes=16 * 1024 * 1024),
        cost_estimate=pl.CostEstimate(flops=rows * columns * 4, bytes_accessed=rows * columns * 6, transcendentals=0),
    )(total, inverse, cosine, sine_part)


def along_x(values, step):
    pairs = [(s, ((s // 2 + step) % 4) * 2 + s % 2) for s in range(N_TENSOR)]
    return lax.ppermute(values, "tensor", pairs)


def across_y(values):
    return lax.ppermute(values, "tensor", [(s, s ^ 1) for s in range(N_TENSOR)])


def along_z(values, step):
    pairs = [(s, (s // 16) * 16 + ((s // 2 + step) % 8) * 2 + s % 2) for s in range(N_POOL)]
    return lax.ppermute(values, "pool", pairs)


def across_low_y(values):
    return lax.ppermute(values, "pool", [(s, s ^ 16) for s in range(N_POOL)])


def across_cores(values):
    return lax.ppermute(values, "pool", [(s, s ^ 1) for s in range(N_POOL)])


def gather_weights(w_key, w_value, pool_index):
    core, z_index, low_y = pool_index % 2, (pool_index // 2) % 8, pool_index // 16
    first = core == 0
    mine = jnp.where(first, w_key, w_value)
    got = across_cores(jnp.where(first, w_value, w_key))
    pair = jnp.concatenate([jnp.where(first, mine, got), jnp.where(first, got, mine)], axis=0)
    half = pair.shape[0] // 2
    below, above = [pair], [pair]
    for _ in range(3):
        below.append(along_z(below[-1], 1))
        above.append(along_z(above[-1], -1))
    far = jnp.concatenate([along_z(below[3][:half], 1), along_z(above[3][half:], -1)], axis=0)
    near = jnp.stack([pair, below[1], above[1], below[2], above[2]])
    rest = jnp.stack([below[3], above[3], far])
    near_y, rest_y = across_low_y(near), across_low_y(rest)
    column = jnp.concatenate([near, rest, near_y, rest_y], axis=0)
    traded = across_cores(column)
    both = jnp.concatenate([column, traded], axis=0)
    place = jnp.array([0, 2, 4, 6, 7, 5, 3, 1], dtype=jnp.int32)
    chip = jnp.arange(CHIPS, dtype=jnp.int32)
    order = place[(chip % 8 - z_index + 8) % 8] + jnp.where(chip // 8 == low_y, 0, 8)
    key_part = both[order + jnp.where(first, 0, CHIPS)]
    value_part = both[order + jnp.where(first, CHIPS, 0)]
    return jnp.concatenate([key_part, value_part], axis=2).reshape(D, 2 * w_key.shape[1])


def gather_rows(own, part, x_index, y_index):
    sources = [x_index, (x_index + 3) % 4, (x_index + 1) % 4, (x_index + 2) % 4]
    part_a, part_b = own[:part], own[part:]
    rows_b = part_b.shape[0]
    other_b = across_y(part_b)
    a_before, a_after = along_x(part_a, 1), along_x(part_a, -1)
    near_a = across_y(jnp.concatenate([part_a, a_before, a_after], axis=0))
    two_b = jnp.concatenate([part_b, other_b], axis=0)
    b_before, b_after = along_x(two_b, 1), along_x(two_b, -1)
    half = part // 2
    a_far = jnp.concatenate([along_x(a_before[:half], 1), along_x(a_after[half:], -1)], axis=0)
    far_a = across_y(a_far)
    b_far = [along_x(b_before[:rows_b], 1), along_x(b_after[rows_b:], -1)]
    pieces_a = [(part_a, 0, 0), (a_before, 1, 0), (a_after, 2, 0), (a_far, 3, 0)]
    pieces_a += [(near_a[k * part : (k + 1) * part], k, 1) for k in range(3)] + [(far_a, 3, 1)]
    pieces_b = [(part_b, 0, 0), (other_b, 0, 1)]
    for k, values in ((1, b_before), (2, b_after)):
        pieces_b += [(values[:rows_b], k, 0), (values[rows_b:], k, 1)]
    pieces_b += [(b_far[0], 3, 0), (b_far[1], 3, 1)]

    def named(pieces):
        return [(v, sources[k] * 2 + (y_index if across == 0 else 1 - y_index)) for v, k, across in pieces]

    return named(pieces_a), named(pieces_b)


def project(pieces, weights, gain_wide):
    slice_width = D // N_TENSOR
    total, squares = None, None
    for values, source in pieces:
        wide = values.astype(jnp.float32)
        gain = lax.dynamic_slice_in_dim(gain_wide, source * slice_width, slice_width)
        share = lax.dynamic_slice_in_dim(weights, source * slice_width, slice_width, axis=0)
        scaled = (wide * gain).astype(jnp.bfloat16)
        part = jnp.dot(scaled, share, preferred_element_type=jnp.float32)
        square = jnp.sum(wide * wide, axis=1)
        total = part if total is None else total + part
        squares = square if squares is None else squares + square
    return total, squares


def shards(
    saved_rows,
    norm_gain,
    w_key,
    w_value,
    req_blocks,
    req_tail,
    group_request,
    owner_table,
    new_hidden,
    queries,
    cache_key,
    cache_value,
    cache_len,
):
    slice_width = saved_rows.shape[1]
    head_width = w_key.shape[1]
    pool_index = lax.axis_index("pool")
    tensor_index = lax.axis_index("tensor")
    core, chip = pool_index % 2, pool_index // 2
    x_index, y_index = tensor_index // 2, tensor_index % 2
    gain_wide = norm_gain.astype(jnp.float32)

    spread = saved_rows.reshape(REQS, CHIPS, UNIT, slice_width).transpose(1, 0, 2, 3)
    same_core = [[2 * k + c for k in range(CHIPS)] for c in range(2)]
    incoming = lax.all_to_all(
        spread.reshape(CHIPS, REQS * UNIT, slice_width),
        "pool",
        split_axis=0,
        concat_axis=0,
        axis_index_groups=same_core,
        tiled=True,
    ).reshape(CHIPS * REQS, UNIT, slice_width)
    weights = gather_weights(w_key, w_value, pool_index)

    by_core = owner_table.reshape(REQS, PAIRS, 2)
    my_owner = jnp.where(core == 0, by_core[:, :, 0], by_core[:, :, 1])
    their_owner = jnp.where(core == 0, by_core[:, :, 1], by_core[:, :, 0])
    slot = jnp.arange(REQS, dtype=jnp.int32)[:, None]
    my_unit = jnp.clip((my_owner // 2) * REQS + slot, 0, CHIPS * REQS - 1)
    their_unit = jnp.clip((their_owner // 2) * REQS + slot, 0, CHIPS * REQS - 1)
    here = my_owner % 2 == core
    lengths = (req_blocks - 1) * BLOCK + req_tail
    inner = jnp.arange(PAIRS, dtype=jnp.int32) * 2 + core
    position = (inner * BLOCK + chip * UNIT)[:, None] + jnp.arange(UNIT, dtype=jnp.int32)[None, :]
    live = position[None] < lengths[:, None, None]
    cosine, sine_part = turn_table(position)
    incoming, my_unit, their_unit, here, live, cosine, sine_part = lax.optimization_barrier(
        (incoming, my_unit, their_unit, here, live, cosine, sine_part)
    )

    local_count, step_count = (new_hidden.shape[0], new_hidden.shape[1])
    tokens = local_count * step_count
    token_rows = jnp.concatenate(
        [new_hidden.reshape(tokens, slice_width), jnp.zeros((tokens, slice_width), jnp.bfloat16)], axis=0
    )
    wanted = group_request[pool_index]
    chosen = jnp.minimum(group_request, REQS - 1)
    arrived_chunks = []
    for chunk, (low, high) in enumerate(CHUNKS):
        count = high - low
        rows = REQS * count * UNIT
        for_them = jnp.take(incoming, their_unit[:, low:high].reshape(-1), axis=0, mode="clip")
        for_me = jnp.take(incoming, my_unit[:, low:high].reshape(-1), axis=0, mode="clip")
        from_them = across_cores(for_them)
        own = jnp.where(here[:, low:high].reshape(-1, 1, 1), for_me, from_them).reshape(rows, slice_width)
        if chunk == 0:
            own = jnp.concatenate([own, token_rows], axis=0)
        pieces_a, pieces_b = gather_rows(own, PART_A[chunk], x_index, y_index)
        sum_a, squares_a = project(pieces_a, weights, gain_wide)
        sum_b, squares_b = project(pieces_b, weights, gain_wide)
        both = jnp.concatenate([sum_a, sum_b], axis=0)
        inverse = lax.rsqrt(jnp.concatenate([squares_a, squares_b]) / D + epsilon)
        if chunk == 0:
            token_both = both[rows : rows + tokens] * inverse[rows : rows + tokens, None]

        def table(part):
            return jnp.broadcast_to(part[None, low:high], (REQS, count, UNIT, HEAD_DIM)).reshape(rows, HEAD_DIM)

        masked = jnp.where(live[:, low:high].reshape(rows), inverse[:rows], 0.0)[:, None]
        restored = finish(both[:rows], masked, table(cosine), table(sine_part))
        outgoing = jnp.take(restored.reshape(REQS, count * UNIT, 2 * head_width), chosen, axis=0, mode="clip")
        arrived = lax.all_to_all(outgoing, "pool", split_axis=0, concat_axis=0, tiled=True)
        arrived = arrived.reshape(CHIPS, 2, count, UNIT, 2 * head_width).transpose(2, 1, 0, 3, 4)
        arrived = arrived.reshape(2 * count * BLOCK, 2 * head_width)
        arrived_chunks.append(jnp.where(wanted < REQS, arrived, jnp.zeros((), jnp.bfloat16)))
    restored_key = jnp.concatenate([part[:, :head_width] for part in arrived_chunks], axis=0)
    restored_value = jnp.concatenate([part[:, head_width:] for part in arrived_chunks], axis=0)

    token_both = token_both.reshape(local_count, step_count, 2 * head_width)
    positions = cache_len[:, None] + jnp.arange(step_count, dtype=jnp.int32)[None, :]
    token_cosine, token_sine = turn_table(positions)
    new_key = rotate(token_both[..., :head_width], token_cosine, token_sine).astype(jnp.bfloat16)
    new_value = token_both[..., head_width:].astype(jnp.bfloat16)
    decode_out = attend(queries, cache_key, cache_value, new_key, new_value, cache_len)
    return (restored_key, restored_value, decode_out, new_key, new_value)


def attend(queries, cache_key, cache_value, fresh_key, fresh_value, cache_len):
    local_count, step_count, feature_count = queries.shape
    head_count = feature_count // HEAD_DIM
    context = cache_key.shape[1]
    score_scale = HEAD_DIM ** (-0.5)
    query_heads = queries.reshape(local_count, step_count, head_count, HEAD_DIM)
    cached_heads = cache_key.reshape(local_count, context, head_count, HEAD_DIM)
    cached_scores = (
        jnp.einsum("rshd,rchd->rshc", query_heads, cached_heads, preferred_element_type=jnp.float32)
        * score_scale
    )
    cached_scores = jnp.where(
        jnp.arange(context)[None, None, None, :] < cache_len[:, None, None, None],
        cached_scores,
        -1e30,
    )
    fresh_heads = fresh_key.reshape(local_count, step_count, head_count, HEAD_DIM)
    fresh_scores = (
        jnp.einsum("rshd,rthd->rsht", query_heads, fresh_heads, preferred_element_type=jnp.float32)
        * score_scale
    )
    causal_mask = jnp.arange(step_count)[None, :] <= jnp.arange(step_count)[:, None]
    fresh_scores = jnp.where(causal_mask[None, :, None, :], fresh_scores, -1e30)
    peak_score = jnp.maximum(jnp.max(cached_scores, axis=-1), jnp.max(fresh_scores, axis=-1))
    cached_terms = jnp.exp(cached_scores - peak_score[..., None])
    fresh_terms = jnp.exp(fresh_scores - peak_score[..., None])
    weight_sum = jnp.sum(cached_terms, axis=-1) + jnp.sum(fresh_terms, axis=-1)
    cached_weights = (cached_terms / weight_sum[..., None]).astype(jnp.bfloat16)
    fresh_weights = (fresh_terms / weight_sum[..., None]).astype(jnp.bfloat16)
    cached_values = cache_value.reshape(local_count, context, head_count, HEAD_DIM)
    fresh_values = fresh_value.reshape(local_count, step_count, head_count, HEAD_DIM)
    output = jnp.einsum(
        "rshc,rchd->rshd", cached_weights, cached_values, preferred_element_type=jnp.float32
    )
    output = output + jnp.einsum(
        "rsht,rthd->rshd", fresh_weights, fresh_values, preferred_element_type=jnp.float32
    )
    return output.reshape(local_count, step_count, feature_count).astype(jnp.bfloat16)


def solution(mesh):
    return jax.shard_map(
        shards,
        mesh=mesh,
        in_specs=(
            P("pool", "tensor"),
            P(),
            P("pool", "tensor"),
            P("pool", "tensor"),
            P(),
            P(),
            P(),
            P(),
            P("pool", None, "tensor"),
            P("pool", None, "tensor"),
            P("pool", None, "tensor"),
            P("pool", None, "tensor"),
            P("pool"),
        ),
        out_specs=(
            P("pool", "tensor"),
            P("pool", "tensor"),
            P("pool", None, "tensor"),
            P("pool", None, "tensor"),
            P("pool", None, "tensor"),
        ),
        check_vma=False,
    )
```

```python
import jax
import jax.numpy as jnp
from jax import lax
from jax.experimental import pallas as pl
from jax.experimental.pallas import tpu as pltpu
from jax.sharding import PartitionSpec as P

D = 5120
HEAD_DIM = 128
REQS = 16
BLOCK = 128
BLOCKS = 208
GBLK = 14
N_POOL = 32
N_TENSOR = 8
SLICE = D // N_TENSOR
SHARE = BLOCK // N_POOL
ROWS = BLOCKS * SHARE
SLOT = GBLK * SHARE
TOKENS = 16
X_FIRST = 208
KEPT = REQS * SLOT


epsilon = 1e-05


def turn_table(positions):
    half_dim = HEAD_DIM // 2
    frequency = 10000.0 ** (-2.0 * jnp.arange(half_dim, dtype=jnp.float32) / HEAD_DIM)
    angle_rows = positions.astype(jnp.float32)[..., None] * frequency
    cosine, sine_part = jnp.cos(angle_rows), jnp.sin(angle_rows)
    return jnp.concatenate([cosine, cosine], axis=-1), jnp.concatenate([-sine_part, sine_part], axis=-1)


def add_slices(steps, source_ref, gain_ref, weight_ref, pieces_of, scaled_ref, total_ref, squares_ref, begun):
    for step in steps:
        source = source_ref[step]
        gain = gain_ref[source]
        begin = 0
        for piece in pieces_of(step):
            end = begin + piece.shape[0]
            wide = piece.astype(jnp.float32)
            square = wide * wide
            lanes = square[:, :128]
            for low in range(128, SLICE, 128):
                lanes = lanes + square[:, low : low + 128]
            squares_ref[begin:end, :] = squares_ref[begin:end, :] + lanes if begun else lanes
            scaled_ref[begin:end, :] = (wide * gain).astype(jnp.bfloat16)
            begin = end
        part = jnp.dot(scaled_ref[...], weight_ref[source], preferred_element_type=jnp.float32)
        total_ref[:begin, :] = total_ref[:begin, :] + part if begun else part
        begun = True


def near_kernel(
    source_ref,
    near_ref,
    near_across_ref,
    two_ref,
    before_ref,
    after_ref,
    gain_ref,
    weight_ref,
    total_ref,
    squares_ref,
    scaled_ref,
):
    low_rows = two_ref.shape[0] // 2
    top = total_ref.shape[0] - low_rows

    def pieces_of(step):
        offset, across = step // 2, step % 2
        upper = (near_across_ref if across else near_ref)[offset * top : (offset + 1) * top, :]
        lower = (two_ref, before_ref, after_ref)[offset][across * low_rows : (across + 1) * low_rows, :]
        return upper, lower

    add_slices(range(6), source_ref, gain_ref, weight_ref, pieces_of, scaled_ref, total_ref, squares_ref, False)


def far_kernel(
    source_ref,
    start_ref,
    count_ref,
    far_ref,
    far_across_ref,
    two_far_ref,
    gain_ref,
    weight_ref,
    begun_ref,
    begun_squares_ref,
    live_ref,
    cosine_ref,
    sine_ref,
    out_ref,
    fresh_ref,
    scaled_ref,
    total_ref,
    squares_ref,
):
    rows, columns = begun_ref.shape
    low_rows = two_far_ref.shape[0] // 2
    total_ref[:rows, :] = begun_ref[...]
    total_ref[rows:, :] = jnp.zeros((KEPT - rows, columns), jnp.float32)
    squares_ref[...] = begun_squares_ref[...]

    def pieces_of(step):
        across = step % 2
        upper = (far_across_ref if across else far_ref)[...]
        return upper, two_far_ref[across * low_rows : (across + 1) * low_rows, :]

    add_slices(range(6, 8), source_ref, gain_ref, weight_ref, pieces_of, scaled_ref, total_ref, squares_ref, True)
    inverse = lax.rsqrt(jnp.sum(squares_ref[...], axis=1, keepdims=True) / D + epsilon) * live_ref[...]
    cosine, sine_part = cosine_ref[...], sine_ref[...]
    for low in range(0, columns, HEAD_DIM):
        one = total_ref[:rows, low : low + HEAD_DIM] * inverse
        if low < columns // 2:
            one = one * cosine + pltpu.roll(one, HEAD_DIM // 2, 1) * sine_part
        total_ref[:rows, low : low + HEAD_DIM] = one
    fresh_ref[...] = total_ref[ROWS : ROWS + TOKENS, :].astype(jnp.bfloat16)

    def send(group, carry):
        start = start_ref[group]
        tile = start // 8
        window = total_ref[pl.ds(pl.multiple_of(tile * 8, 8), SLOT + 8), :]
        mine = jnp.where(start == tile * 8, window[:SLOT], window[SHARE : SHARE + SLOT])
        line = lax.broadcasted_iota(jnp.int32, (SLOT, columns), 0)
        out_ref[group] = jnp.where(line < count_ref[group], mine, 0.0).astype(jnp.bfloat16)
        return carry

    lax.fori_loop(0, N_POOL, send, 0)


def project(sources, starts, counts, pieces, weights, gain_wide, live, cosine, sine_part):
    near, far, near_across, far_across, two, two_before, two_after, two_far = pieces
    rows = live.shape[0]
    columns = weights.shape[2]
    whole = pl.BlockSpec(memory_space=pltpu.VMEM)
    numbers = pl.BlockSpec(memory_space=pltpu.SMEM)
    total, squares = pl.pallas_call(
        near_kernel,
        out_shape=(
            jax.ShapeDtypeStruct((rows, columns), jnp.float32),
            jax.ShapeDtypeStruct((rows, 128), jnp.float32),
        ),
        in_specs=[numbers] + [whole] * 7,
        out_specs=(whole, whole),
        scratch_shapes=[pltpu.VMEM((rows, SLICE), jnp.bfloat16)],
        compiler_params=pltpu.CompilerParams(vmem_limit_bytes=40 * 1024 * 1024),
        cost_estimate=pl.CostEstimate(
            flops=3 * rows * D * columns // 2, bytes_accessed=2 * D * (rows + columns), transcendentals=0
        ),
    )(sources, near, near_across, two, two_before, two_after, gain_wide, weights)
    return pl.pallas_call(
        far_kernel,
        out_shape=(
            jax.ShapeDtypeStruct((N_POOL, SLOT, columns), jnp.bfloat16),
            jax.ShapeDtypeStruct((TOKENS, columns), jnp.bfloat16),
        ),
        in_specs=[numbers] * 3 + [whole] * 10,
        out_specs=(whole, whole),
        scratch_shapes=[
            pltpu.VMEM((rows, SLICE), jnp.bfloat16),
            pltpu.VMEM((KEPT, columns), jnp.float32),
            pltpu.VMEM((rows, 128), jnp.float32),
        ],
        compiler_params=pltpu.CompilerParams(vmem_limit_bytes=40 * 1024 * 1024),
        cost_estimate=pl.CostEstimate(
            flops=rows * D * columns // 2, bytes_accessed=D * (rows + columns), transcendentals=0
        ),
    )(
        sources, starts, counts, far, far_across, two_far, gain_wide, weights, total, squares, live, cosine, sine_part
    )


def pick_rows(index, table):
    chosen = (index[:, None] == jnp.arange(table.shape[0], dtype=jnp.int32)[None, :]).astype(jnp.bfloat16)
    return jnp.dot(chosen, table, preferred_element_type=jnp.float32).astype(jnp.bfloat16)


def along_x(values, step):
    pairs = [(s, ((s // 2 + step) % 4) * 2 + s % 2) for s in range(N_TENSOR)]
    return lax.ppermute(values, "tensor", pairs)


def across_y(values):
    return lax.ppermute(values, "tensor", [(s, s ^ 1) for s in range(N_TENSOR)])


def far_x(before, after, rows):
    return jnp.concatenate([along_x(before[:rows], 1), along_x(after[rows:], -1)], axis=0)


def gather_rows(own):
    upper, lower = own[:X_FIRST], own[X_FIRST:]
    other = across_y(lower)
    before, after = along_x(upper, 1), along_x(upper, -1)
    other, before, after = lax.optimization_barrier((other, before, after))
    near = jnp.concatenate([upper, before, after], axis=0)
    two = jnp.concatenate([lower, other], axis=0)
    far = far_x(before, after, X_FIRST // 2)
    two_before, two_after = along_x(two, 1), along_x(two, -1)
    near_across = across_y(near)
    far, two_before, two_after, near_across = lax.optimization_barrier((far, two_before, two_after, near_across))
    far_across = across_y(far)
    two_far = far_x(two_before, two_after, lower.shape[0])
    return near, far, near_across, far_across, two, two_before, two_after, two_far


def shards(
    saved_rows,
    norm_gain,
    w_key,
    w_value,
    req_blocks,
    req_tail,
    group_request,
    owner_table,
    new_hidden,
    queries,
    cache_key,
    cache_value,
    cache_len,
):
    slice_width = saved_rows.shape[1]
    head_width = w_key.shape[1]
    pool_index = lax.axis_index("pool")
    tensor_index = lax.axis_index("tensor")
    x_index, y_index = tensor_index // 2, tensor_index % 2
    gain_wide = norm_gain.astype(jnp.float32).reshape(N_TENSOR, 1, SLICE)
    order = jnp.stack([x_index, (x_index + 3) % 4, (x_index + 1) % 4, (x_index + 2) % 4]).astype(jnp.int32)
    sources = jnp.stack([order * 2 + y_index, order * 2 + 1 - y_index], axis=1).reshape(-1)

    slot = jnp.arange(REQS, dtype=jnp.int32)
    inside = jnp.arange(SHARE, dtype=jnp.int32)
    tiles = saved_rows.reshape(REQS, N_POOL // 2, 2 * SHARE, slice_width).transpose(1, 0, 2, 3)
    tiles = tiles.reshape(N_POOL // 2, REQS * 2 * SHARE, slice_width)
    line = jnp.arange(REQS * 2 * SHARE, dtype=jnp.int32)
    half = REQS * SHARE
    away = (line % half) // SHARE * (2 * SHARE) + line // half * SHARE + line % SHARE
    away = (away[:, None] == line[None, :]).astype(jnp.bfloat16)
    spread = jnp.einsum("ab,qbc->qac", away, tiles, preferred_element_type=jnp.float32).astype(jnp.bfloat16)
    spread = spread.reshape(N_POOL, REQS * SHARE, slice_width)
    incoming = lax.all_to_all(spread, "pool", split_axis=0, concat_axis=0, tiled=True)

    local_count, step_count = (new_hidden.shape[0], new_hidden.shape[1])
    tokens = local_count * step_count
    ends = jnp.cumsum(req_blocks)
    starts = ends - req_blocks
    count = jnp.arange(BLOCKS, dtype=jnp.int32)
    member = (count[:, None] >= starts[None, :]) & (count[:, None] < ends[None, :])
    request = jnp.sum(jnp.where(member, slot[None, :], 0), axis=1)
    inner = count - jnp.sum(jnp.where(member, starts[None, :], 0), axis=1)
    length = jnp.sum(jnp.where(member, ((req_blocks - 1) * BLOCK + req_tail)[None, :], 0), axis=1)
    at = (request * GBLK + inner)[:, None] == jnp.arange(REQS * GBLK, dtype=jnp.int32)[None, :]
    owner = jnp.sum(jnp.where(at, owner_table.reshape(1, -1), 0), axis=1)
    my_rows = ((owner * REQS + request)[:, None] * SHARE + inside).reshape(-1)
    position = ((inner * BLOCK + pool_index * SHARE)[:, None] + inside).reshape(-1)
    live = (position < jnp.repeat(length, SHARE)).astype(jnp.float32)
    token_position = (cache_len[:, None] + jnp.arange(step_count, dtype=jnp.int32)[None, :]).reshape(-1)
    position = jnp.concatenate([position, token_position, token_position])
    live = jnp.concatenate([live, jnp.ones((TOKENS,), jnp.float32)])[:, None]
    cosine, sine_part = turn_table(position)

    holder = (group_request[:, None] == slot[None, :]).astype(jnp.int32)
    group_start = jnp.sum(holder * starts[None, :], axis=1) * SHARE
    group_rows = jnp.sum(holder * req_blocks[None, :], axis=1) * SHARE
    incoming, my_rows, live, cosine, sine_part, group_start, group_rows = lax.optimization_barrier(
        (incoming, my_rows, live, cosine, sine_part, group_start, group_rows)
    )

    paired = jnp.concatenate([w_key, w_value], axis=1)
    paired, incoming = lax.optimization_barrier((paired, incoming))
    weights = lax.all_gather(paired, "pool", axis=0, tiled=True).reshape(N_TENSOR, SLICE, 2 * head_width)
    token_rows = jnp.concatenate(
        [new_hidden.reshape(tokens, slice_width), jnp.zeros((TOKENS - tokens, slice_width), jnp.bfloat16)], axis=0
    )
    own = pick_rows(my_rows, incoming.reshape(N_POOL * REQS * SHARE, slice_width))
    own = jnp.concatenate([own, token_rows], axis=0)
    outgoing, fresh = project(
        sources, group_start, group_rows, gather_rows(own), weights, gain_wide, live, cosine, sine_part
    )
    arrived = lax.all_to_all(outgoing, "pool", split_axis=0, concat_axis=0, tiled=True)
    pairs = arrived.reshape(N_POOL, GBLK // 2, 2 * SHARE, 2 * head_width).transpose(1, 0, 2, 3)
    pairs = pairs.reshape(GBLK // 2, 2 * BLOCK, 2 * head_width)
    line = jnp.arange(2 * BLOCK, dtype=jnp.int32)
    home = (line % BLOCK) // SHARE * (2 * SHARE) + line // BLOCK * SHARE + line % SHARE
    home = (home[:, None] == line[None, :]).astype(jnp.bfloat16)

    def in_order(part):
        ordered = jnp.einsum("ab,ibc->iac", home, part, preferred_element_type=jnp.float32)
        return ordered.astype(jnp.bfloat16).reshape(GBLK * BLOCK, head_width)

    restored_key = in_order(pairs[..., :head_width])
    restored_value = in_order(pairs[..., head_width:])
    fresh = fresh[:tokens].reshape(local_count, step_count, 2 * head_width)
    new_key, new_value = fresh[..., :head_width], fresh[..., head_width:]
    decode_out = attend(queries, cache_key, cache_value, new_key, new_value, cache_len)
    return (restored_key, restored_value, decode_out, new_key, new_value)


def attend(queries, cache_key, cache_value, fresh_key, fresh_value, cache_len):
    local_count, step_count, feature_count = queries.shape
    head_count = feature_count // HEAD_DIM
    context = cache_key.shape[1]
    score_scale = HEAD_DIM ** (-0.5)
    query_heads = queries.reshape(local_count, step_count, head_count, HEAD_DIM)
    cached_heads = cache_key.reshape(local_count, context, head_count, HEAD_DIM)
    cached_scores = (
        jnp.einsum("rshd,rchd->rshc", query_heads, cached_heads, preferred_element_type=jnp.float32)
        * score_scale
    )
    cached_scores = jnp.where(
        jnp.arange(context)[None, None, None, :] < cache_len[:, None, None, None],
        cached_scores,
        -1e30,
    )
    fresh_heads = fresh_key.reshape(local_count, step_count, head_count, HEAD_DIM)
    fresh_scores = (
        jnp.einsum("rshd,rthd->rsht", query_heads, fresh_heads, preferred_element_type=jnp.float32)
        * score_scale
    )
    causal_mask = jnp.arange(step_count)[None, :] <= jnp.arange(step_count)[:, None]
    fresh_scores = jnp.where(causal_mask[None, :, None, :], fresh_scores, -1e30)
    peak_score = jnp.maximum(jnp.max(cached_scores, axis=-1), jnp.max(fresh_scores, axis=-1))
    cached_terms = jnp.exp(cached_scores - peak_score[..., None])
    fresh_terms = jnp.exp(fresh_scores - peak_score[..., None])
    weight_sum = jnp.sum(cached_terms, axis=-1) + jnp.sum(fresh_terms, axis=-1)
    cached_weights = (cached_terms / weight_sum[..., None]).astype(jnp.bfloat16)
    fresh_weights = (fresh_terms / weight_sum[..., None]).astype(jnp.bfloat16)
    cached_values = cache_value.reshape(local_count, context, head_count, HEAD_DIM)
    fresh_values = fresh_value.reshape(local_count, step_count, head_count, HEAD_DIM)
    output = jnp.einsum(
        "rshc,rchd->rshd", cached_weights, cached_values, preferred_element_type=jnp.float32
    )
    output = output + jnp.einsum(
        "rsht,rthd->rshd", fresh_weights, fresh_values, preferred_element_type=jnp.float32
    )
    return output.reshape(local_count, step_count, feature_count).astype(jnp.bfloat16)


def solution(mesh):
    return jax.shard_map(
        shards,
        mesh=mesh,
        in_specs=(
            P("pool", "tensor"),
            P(),
            P("pool", "tensor"),
            P("pool", "tensor"),
            P(),
            P(),
            P(),
            P(),
            P("pool", None, "tensor"),
            P("pool", None, "tensor"),
            P("pool", None, "tensor"),
            P("pool", None, "tensor"),
            P("pool"),
        ),
        out_specs=(
            P("pool", "tensor"),
            P("pool", "tensor"),
            P("pool", None, "tensor"),
            P("pool", None, "tensor"),
            P("pool", None, "tensor"),
        ),
        check_vma=False,
    )
```

```python
import jax
import jax.numpy as jnp
from jax import lax
from jax.experimental import pallas as pl
from jax.experimental.pallas import tpu as pltpu
from jax.sharding import PartitionSpec as P

D = 5120
HEAD_DIM = 128
REQS = 16
BLOCK = 128
BLOCKS = 208
GBLK = 14
N_POOL = 32
N_TENSOR = 8
SLICE = D // N_TENSOR
SHARE = BLOCK // N_POOL
ROWS = BLOCKS * SHARE
SLOT = GBLK * SHARE
TOKENS = 16
X_FIRST = 208
KEPT = REQS * SLOT


epsilon = 1e-05


def turn_table(positions):
    half_dim = HEAD_DIM // 2
    frequency = 10000.0 ** (-2.0 * jnp.arange(half_dim, dtype=jnp.float32) / HEAD_DIM)
    angle_rows = positions.astype(jnp.float32)[..., None] * frequency
    cosine, sine_part = jnp.cos(angle_rows), jnp.sin(angle_rows)
    return jnp.concatenate([cosine, cosine], axis=-1), jnp.concatenate([-sine_part, sine_part], axis=-1)


def add_slices(steps, source_ref, gain_ref, weight_ref, pieces_of, scaled_ref, total_ref, squares_ref, begun):
    for step in steps:
        source = source_ref[step]
        gain = gain_ref[source]
        begin = 0
        for piece in pieces_of(step):
            end = begin + piece.shape[0]
            wide = piece.astype(jnp.float32)
            square = wide * wide
            lanes = square[:, :128]
            for low in range(128, SLICE, 128):
                lanes = lanes + square[:, low : low + 128]
            squares_ref[begin:end, :] = squares_ref[begin:end, :] + lanes if begun else lanes
            scaled_ref[begin:end, :] = (wide * gain).astype(jnp.bfloat16)
            begin = end
        part = jnp.dot(scaled_ref[...], weight_ref[source], preferred_element_type=jnp.float32)
        total_ref[:begin, :] = total_ref[:begin, :] + part if begun else part
        begun = True


def near_kernel(
    source_ref,
    near_ref,
    near_across_ref,
    lower_ref,
    lower_across_ref,
    before_ref,
    before_across_ref,
    after_ref,
    after_across_ref,
    gain_ref,
    weight_ref,
    total_ref,
    squares_ref,
    scaled_ref,
):
    top = near_ref.shape[0] // 3
    lower = (lower_ref, lower_across_ref, before_ref, before_across_ref, after_ref, after_across_ref)

    def pieces_of(step):
        offset, across = step // 2, step % 2
        upper = (near_across_ref if across else near_ref)[offset * top : (offset + 1) * top, :]
        return upper, lower[step][...]

    add_slices(range(6), source_ref, gain_ref, weight_ref, pieces_of, scaled_ref, total_ref, squares_ref, False)


def far_kernel(
    source_ref,
    start_ref,
    count_ref,
    far_ref,
    far_across_ref,
    low_first_ref,
    low_second_ref,
    across_first_ref,
    across_second_ref,
    gain_ref,
    weight_ref,
    begun_ref,
    begun_squares_ref,
    live_ref,
    cosine_ref,
    sine_ref,
    out_ref,
    fresh_ref,
    scaled_ref,
    total_ref,
    squares_ref,
):
    rows, columns = begun_ref.shape
    total_ref[:rows, :] = begun_ref[...]
    total_ref[rows:, :] = jnp.zeros((KEPT - rows, columns), jnp.float32)
    squares_ref[...] = begun_squares_ref[...]

    def pieces_of(step):
        if step % 2:
            return far_across_ref[...], across_first_ref[...], across_second_ref[...]
        return far_ref[...], low_first_ref[...], low_second_ref[...]

    add_slices(range(6, 8), source_ref, gain_ref, weight_ref, pieces_of, scaled_ref, total_ref, squares_ref, True)
    inverse = lax.rsqrt(jnp.sum(squares_ref[...], axis=1, keepdims=True) / D + epsilon) * live_ref[...]
    cosine, sine_part = cosine_ref[...], sine_ref[...]
    for low in range(0, columns, HEAD_DIM):
        one = total_ref[:rows, low : low + HEAD_DIM] * inverse
        if low < columns // 2:
            one = one * cosine + pltpu.roll(one, HEAD_DIM // 2, 1) * sine_part
        total_ref[:rows, low : low + HEAD_DIM] = one
    fresh_ref[...] = total_ref[ROWS : ROWS + TOKENS, :].astype(jnp.bfloat16)

    def send(group, carry):
        start = start_ref[group]
        tile = start // 8
        window = total_ref[pl.ds(pl.multiple_of(tile * 8, 8), SLOT + 8), :]
        mine = jnp.where(start == tile * 8, window[:SLOT], window[SHARE : SHARE + SLOT])
        line = lax.broadcasted_iota(jnp.int32, (SLOT, columns), 0)
        out_ref[group] = jnp.where(line < count_ref[group], mine, 0.0).astype(jnp.bfloat16)
        return carry

    lax.fori_loop(0, N_POOL, send, 0)


def project(sources, starts, counts, pieces, weights, gain_wide, live, cosine, sine_part):
    near_pieces, far_pieces = pieces
    rows = live.shape[0]
    columns = weights.shape[2]
    whole = pl.BlockSpec(memory_space=pltpu.VMEM)
    numbers = pl.BlockSpec(memory_space=pltpu.SMEM)
    total, squares = pl.pallas_call(
        near_kernel,
        out_shape=(
            jax.ShapeDtypeStruct((rows, columns), jnp.float32),
            jax.ShapeDtypeStruct((rows, 128), jnp.float32),
        ),
        in_specs=[numbers] + [whole] * 10,
        out_specs=(whole, whole),
        scratch_shapes=[pltpu.VMEM((rows, SLICE), jnp.bfloat16)],
        compiler_params=pltpu.CompilerParams(vmem_limit_bytes=40 * 1024 * 1024),
        cost_estimate=pl.CostEstimate(
            flops=3 * rows * D * columns // 2, bytes_accessed=2 * D * (rows + columns), transcendentals=0
        ),
    )(sources, *near_pieces, gain_wide, weights)
    return pl.pallas_call(
        far_kernel,
        out_shape=(
            jax.ShapeDtypeStruct((N_POOL, SLOT, columns), jnp.bfloat16),
            jax.ShapeDtypeStruct((TOKENS, columns), jnp.bfloat16),
        ),
        in_specs=[numbers] * 3 + [whole] * 13,
        out_specs=(whole, whole),
        scratch_shapes=[
            pltpu.VMEM((rows, SLICE), jnp.bfloat16),
            pltpu.VMEM((KEPT, columns), jnp.float32),
            pltpu.VMEM((rows, 128), jnp.float32),
        ],
        compiler_params=pltpu.CompilerParams(vmem_limit_bytes=40 * 1024 * 1024),
        cost_estimate=pl.CostEstimate(
            flops=rows * D * columns // 2, bytes_accessed=D * (rows + columns), transcendentals=0
        ),
    )(sources, starts, counts, *far_pieces, gain_wide, weights, total, squares, live, cosine, sine_part)


def pick_rows(index, table):
    chosen = (index[:, None] == jnp.arange(table.shape[0], dtype=jnp.int32)[None, :]).astype(jnp.bfloat16)
    return jnp.dot(chosen, table, preferred_element_type=jnp.float32).astype(jnp.bfloat16)


def along_x(values, step):
    pairs = [(s, ((s // 2 + step) % 4) * 2 + s % 2) for s in range(N_TENSOR)]
    return lax.ppermute(values, "tensor", pairs)


def across_y(values):
    return lax.ppermute(values, "tensor", [(s, s ^ 1) for s in range(N_TENSOR)])


def far_x(before, after):
    half = before.shape[0] // 2
    return along_x(before[:half], 1), along_x(after[half:], -1)


def gather_rows(own, weights):
    upper, lower = own[:X_FIRST], own[X_FIRST:]
    lower_across = across_y(lower)
    upper_before, upper_after = along_x(upper, 1), along_x(upper, -1)
    before, after = along_x(lower, 1), along_x(lower, -1)
    lower_across, upper_before, upper_after, before, after = lax.optimization_barrier(
        (lower_across, upper_before, upper_after, before, after)
    )
    before_across, after_across = along_x(lower_across, 1), along_x(lower_across, -1)
    near = jnp.concatenate([upper, upper_before, upper_after], axis=0)
    near_across = across_y(near)
    far = jnp.concatenate(far_x(upper_before, upper_after), axis=0)
    lower_far = far_x(before, after)
    far, lower_far, before_across, after_across, near_across, weights = lax.optimization_barrier(
        (far, lower_far, before_across, after_across, near_across, weights)
    )
    far_across = across_y(far)
    across_far = far_x(before_across, after_across)
    near_pieces = (near, near_across, lower, lower_across, before, before_across, after, after_across)
    return (near_pieces, (far, far_across, *lower_far, *across_far)), weights


def shards(
    saved_rows,
    norm_gain,
    w_key,
    w_value,
    req_blocks,
    req_tail,
    group_request,
    owner_table,
    new_hidden,
    queries,
    cache_key,
    cache_value,
    cache_len,
):
    slice_width = saved_rows.shape[1]
    head_width = w_key.shape[1]
    pool_index = lax.axis_index("pool")
    tensor_index = lax.axis_index("tensor")
    x_index, y_index = tensor_index // 2, tensor_index % 2
    gain_wide = norm_gain.astype(jnp.float32).reshape(N_TENSOR, 1, SLICE)
    order = jnp.stack([x_index, (x_index + 3) % 4, (x_index + 1) % 4, (x_index + 2) % 4]).astype(jnp.int32)
    sources = jnp.stack([order * 2 + y_index, order * 2 + 1 - y_index], axis=1).reshape(-1)

    slot = jnp.arange(REQS, dtype=jnp.int32)
    inside = jnp.arange(SHARE, dtype=jnp.int32)
    tiles = saved_rows.reshape(REQS, N_POOL // 2, 2 * SHARE, slice_width).transpose(1, 0, 2, 3)
    tiles = tiles.reshape(N_POOL // 2, REQS * 2 * SHARE, slice_width)
    line = jnp.arange(REQS * 2 * SHARE, dtype=jnp.int32)
    half = REQS * SHARE
    away = (line % half) // SHARE * (2 * SHARE) + line // half * SHARE + line % SHARE
    away = (away[:, None] == line[None, :]).astype(jnp.bfloat16)
    spread = jnp.einsum("ab,qbc->qac", away, tiles, preferred_element_type=jnp.float32).astype(jnp.bfloat16)
    spread = spread.reshape(N_POOL, REQS * SHARE, slice_width)
    incoming = lax.all_to_all(spread, "pool", split_axis=0, concat_axis=0, tiled=True)

    local_count, step_count = (new_hidden.shape[0], new_hidden.shape[1])
    tokens = local_count * step_count
    ends = jnp.cumsum(req_blocks)
    starts = ends - req_blocks
    count = jnp.arange(BLOCKS, dtype=jnp.int32)
    member = (count[:, None] >= starts[None, :]) & (count[:, None] < ends[None, :])
    request = jnp.sum(jnp.where(member, slot[None, :], 0), axis=1)
    inner = count - jnp.sum(jnp.where(member, starts[None, :], 0), axis=1)
    length = jnp.sum(jnp.where(member, ((req_blocks - 1) * BLOCK + req_tail)[None, :], 0), axis=1)
    at = (request * GBLK + inner)[:, None] == jnp.arange(REQS * GBLK, dtype=jnp.int32)[None, :]
    owner = jnp.sum(jnp.where(at, owner_table.reshape(1, -1), 0), axis=1)
    my_rows = ((owner * REQS + request)[:, None] * SHARE + inside).reshape(-1)
    position = ((inner * BLOCK + pool_index * SHARE)[:, None] + inside).reshape(-1)
    live = (position < jnp.repeat(length, SHARE)).astype(jnp.float32)
    token_position = (cache_len[:, None] + jnp.arange(step_count, dtype=jnp.int32)[None, :]).reshape(-1)
    position = jnp.concatenate([position, token_position, token_position])
    live = jnp.concatenate([live, jnp.ones((TOKENS,), jnp.float32)])[:, None]
    cosine, sine_part = turn_table(position)

    holder = (group_request[:, None] == slot[None, :]).astype(jnp.int32)
    group_start = jnp.sum(holder * starts[None, :], axis=1) * SHARE
    group_rows = jnp.sum(holder * req_blocks[None, :], axis=1) * SHARE
    incoming, my_rows, live, cosine, sine_part, group_start, group_rows = lax.optimization_barrier(
        (incoming, my_rows, live, cosine, sine_part, group_start, group_rows)
    )

    paired = jnp.concatenate([w_key, w_value], axis=1)
    paired, incoming = lax.optimization_barrier((paired, incoming))
    weights = lax.all_gather(paired, "pool", axis=0, tiled=True).reshape(N_TENSOR, SLICE, 2 * head_width)
    token_rows = jnp.concatenate(
        [new_hidden.reshape(tokens, slice_width), jnp.zeros((TOKENS - tokens, slice_width), jnp.bfloat16)], axis=0
    )
    own = pick_rows(my_rows, incoming.reshape(N_POOL * REQS * SHARE, slice_width))
    own = jnp.concatenate([own, token_rows], axis=0)
    pieces, weights = gather_rows(own, weights)
    outgoing, fresh = project(
        sources, group_start, group_rows, pieces, weights, gain_wide, live, cosine, sine_part
    )
    arrived = lax.all_to_all(outgoing, "pool", split_axis=0, concat_axis=0, tiled=True)
    pairs = arrived.reshape(N_POOL, GBLK // 2, 2 * SHARE, 2 * head_width).transpose(1, 0, 2, 3)
    pairs = pairs.reshape(GBLK // 2, 2 * BLOCK, 2 * head_width)
    line = jnp.arange(2 * BLOCK, dtype=jnp.int32)
    home = (line % BLOCK) // SHARE * (2 * SHARE) + line // BLOCK * SHARE + line % SHARE
    home = (home[:, None] == line[None, :]).astype(jnp.bfloat16)

    def in_order(part):
        ordered = jnp.einsum("ab,ibc->iac", home, part, preferred_element_type=jnp.float32)
        return ordered.astype(jnp.bfloat16).reshape(GBLK * BLOCK, head_width)

    restored_key = in_order(pairs[..., :head_width])
    restored_value = in_order(pairs[..., head_width:])
    fresh = fresh[:tokens].reshape(local_count, step_count, 2 * head_width)
    new_key, new_value = fresh[..., :head_width], fresh[..., head_width:]
    decode_out = attend(queries, cache_key, cache_value, new_key, new_value, cache_len)
    return (restored_key, restored_value, decode_out, new_key, new_value)


def attend(queries, cache_key, cache_value, fresh_key, fresh_value, cache_len):
    local_count, step_count, feature_count = queries.shape
    head_count = feature_count // HEAD_DIM
    context = cache_key.shape[1]
    score_scale = HEAD_DIM ** (-0.5)
    query_heads = queries.reshape(local_count, step_count, head_count, HEAD_DIM)
    cached_heads = cache_key.reshape(local_count, context, head_count, HEAD_DIM)
    cached_scores = (
        jnp.einsum("rshd,rchd->rshc", query_heads, cached_heads, preferred_element_type=jnp.float32)
        * score_scale
    )
    cached_scores = jnp.where(
        jnp.arange(context)[None, None, None, :] < cache_len[:, None, None, None],
        cached_scores,
        -1e30,
    )
    fresh_heads = fresh_key.reshape(local_count, step_count, head_count, HEAD_DIM)
    fresh_scores = (
        jnp.einsum("rshd,rthd->rsht", query_heads, fresh_heads, preferred_element_type=jnp.float32)
        * score_scale
    )
    causal_mask = jnp.arange(step_count)[None, :] <= jnp.arange(step_count)[:, None]
    fresh_scores = jnp.where(causal_mask[None, :, None, :], fresh_scores, -1e30)
    peak_score = jnp.maximum(jnp.max(cached_scores, axis=-1), jnp.max(fresh_scores, axis=-1))
    cached_terms = jnp.exp(cached_scores - peak_score[..., None])
    fresh_terms = jnp.exp(fresh_scores - peak_score[..., None])
    weight_sum = jnp.sum(cached_terms, axis=-1) + jnp.sum(fresh_terms, axis=-1)
    cached_weights = (cached_terms / weight_sum[..., None]).astype(jnp.bfloat16)
    fresh_weights = (fresh_terms / weight_sum[..., None]).astype(jnp.bfloat16)
    cached_values = cache_value.reshape(local_count, context, head_count, HEAD_DIM)
    fresh_values = fresh_value.reshape(local_count, step_count, head_count, HEAD_DIM)
    output = jnp.einsum(
        "rshc,rchd->rshd", cached_weights, cached_values, preferred_element_type=jnp.float32
    )
    output = output + jnp.einsum(
        "rsht,rthd->rshd", fresh_weights, fresh_values, preferred_element_type=jnp.float32
    )
    return output.reshape(local_count, step_count, feature_count).astype(jnp.bfloat16)


def solution(mesh):
    return jax.shard_map(
        shards,
        mesh=mesh,
        in_specs=(
            P("pool", "tensor"),
            P(),
            P("pool", "tensor"),
            P("pool", "tensor"),
            P(),
            P(),
            P(),
            P(),
            P("pool", None, "tensor"),
            P("pool", None, "tensor"),
            P("pool", None, "tensor"),
            P("pool", None, "tensor"),
            P("pool"),
        ),
        out_specs=(
            P("pool", "tensor"),
            P("pool", "tensor"),
            P("pool", None, "tensor"),
            P("pool", None, "tensor"),
            P("pool", None, "tensor"),
        ),
        check_vma=False,
    )
```
